32 devices in a mesh: groups: 2 (over x), context: 16 (over z, y, core).
Axes of the slice: x: 2, y: 2, z: 4, core: 2. Of those that a mesh axis runs over, the one named last changes fastest.
Arguments:
- q_store: bfloat16 [4096, 4096], P(('groups', 'context')), parts along dimension 0, may hold values from -6 to 6
- k_store: bfloat16 [4096, 4096], P(('groups', 'context')), parts along dimension 0, may hold values from -6 to 6
- v_store: bfloat16 [4096, 4096], P(('groups', 'context')), parts along dimension 0, may hold values from -6 to 6
- plan: int32 [32, 128], P(('groups', 'context')), parts along dimension 0, may hold values from 0 to 127, each once within a row
- doc_ids: int32 [4096], P(('groups', 'context')), parts along dimension 0, may hold values from 0 to 3, never falling along the last dimension, each value on 1 to 1024 neighbouring positions
- gain: float32 [4096], replicated, may hold values from 0.5 to 1.5
Outputs:
- out_store: bfloat16 [4096, 4096], P(('groups', 'context')), parts along dimension 0
The draws below stay inside these ranges and needn't reach their ends.
There are 2 independent parts, one for each index of `groups`. The reference program is written for one: setup_inputs(seed, part) draws one part's arguments, and reference() takes and returns one part's arrays. A program takes and returns all parts, laid end to end along the dimension named above; an argument that names none is the same for every part. Nothing has to cross between parts.
Inputs may be any that keep to these rules, and one draw needn't show every extreme that they name: Each row of plan names every offset below 128 once. `doc_ids`: never falls along positions; each document holds 1 to 1024 positions.
All inputs are finite; a program needn't handle non-finite values.
Results may differ from the reference program's by a relative error of at most 0.005.
Values may be sent and summed in bfloat16 or wider, within the bound.
A program may use at most 320 MiB of HBM per device.

```python
import math
import jax
import jax.numpy as jnp
import numpy as np
from jax import lax

HEADS = 32
HEAD_DIM = 128
SPAN = 128
DOCS = 4
TOK_DEV = 128
TOKENS = 2048
N_CONTEXT = 16


def levels(stream_key, extent, cuts, least, largest):
    def one(dim, parts):
        heights = jax.random.uniform(jax.random.fold_in(jax.random.fold_in(stream_key, 6), dim), (parts,), jnp.float32, least / len(cuts), largest / len(cuts))
        return jnp.repeat(jnp.exp(heights), extent[dim] // parts).reshape((-1,) + (1,) * (len(extent) - dim - 1))

    loudness = one(*cuts[0])
    for cut in cuts[1:]:
        loudness = loudness * one(*cut)
    return loudness


def profile(number_of, total, limit, slope):
    weights = [(1 << 20) // math.isqrt(standing ** slope) + 1 for standing in range(2, number_of + 1)]
    spare, given = total - limit - (number_of - 1), [1] * (number_of - 1)
    while spare > 0:
        candidates = [i for i in range(number_of - 1) if given[i] < limit]
        mass, remaining = sum([weights[i] for i in candidates]), spare
        for i in candidates:
            more = min(limit - given[i], max(1, remaining * weights[i] // mass), spare)
            given[i] = given[i] + more
            spare = spare - more
    return np.array([limit] + given)


def ragged(stream_key, count, total, most, slope):
    if count == 2:
        one = jax.random.randint(stream_key, (), max(1, total - most), min(most, total - 1) + 1)
        return jnp.stack([one, total - one])
    sizes = jnp.asarray(profile(count, total, most, slope), jnp.int32)
    couples = (count - 1) // 2
    giver, receiver = sizes[1:1 + 2 * couples:2], sizes[2:2 + 2 * couples:2]
    margin = jnp.minimum(giver - 1, most - receiver)
    moved = jax.random.randint(jax.random.fold_in(stream_key, 1), (couples,), 0, 1 << 20) % (margin + 1)
    sizes = sizes.at[1:1 + 2 * couples:2].set(giver - moved).at[2:2 + 2 * couples:2].set(receiver + moved)
    return sizes[jax.random.permutation(jax.random.fold_in(stream_key, 2), count)]


def gaussian(stream_key, extent, scale, reach, split=(), kind=jnp.bfloat16):
    level = levels(stream_key, extent, split, -0.22, 0.18) if split else 1.0
    values = jax.random.normal(stream_key, extent, jnp.float32) * scale * level
    return jnp.minimum(jnp.maximum(values, -reach), reach).astype(kind)


def setup_inputs(seed: int = 0, part: int = 0) -> dict:
    keys = jax.random.split(jax.random.key(seed), 7)
    own_keys = jax.random.split(jax.random.fold_in(keys[6], part), 7)
    q_store = gaussian(own_keys[0], (TOKENS, HEADS * HEAD_DIM), 1.0, 6.0, ((0, 16),))
    k_store = gaussian(own_keys[1], (TOKENS, HEADS * HEAD_DIM), 1.0, 6.0, ((0, 16),))
    v_store = gaussian(own_keys[2], (TOKENS, HEADS * HEAD_DIM), 1.0, 6.0, ((0, 16),))
    plan = jax.vmap(lambda own: jax.random.permutation(own, TOK_DEV))(jax.random.split(own_keys[3], N_CONTEXT)).reshape((N_CONTEXT, TOK_DEV)).astype(jnp.int32)
    doc_ids = jnp.searchsorted(jnp.cumsum(ragged(own_keys[4], DOCS, TOKENS, TOKENS // 2, 1)), jnp.arange(TOKENS), side="right").astype(jnp.int32)
    gain = jnp.clip(1.0 + 0.1 * jax.random.normal(keys[5], (HEADS * HEAD_DIM,), jnp.float32), 0.5, 1.5)
    return {"q_store": q_store, "k_store": k_store, "v_store": v_store, "plan": plan, "doc_ids": doc_ids, "gain": gain}


def merge_states(earlier, later):
    early_state, early_doc = earlier
    late_state, late_doc = later
    keep_early = jnp.logical_or(early_doc == late_doc, late_doc < 0)
    merged = late_state + jnp.where(keep_early[:, None, None], early_state, jnp.zeros_like(early_state))
    return (merged, jnp.where(late_doc < 0, early_doc, late_doc))

def reference(q_store, k_store, v_store, plan, doc_ids, gain):
    devices = N_CONTEXT
    share = TOK_DEV // N_CONTEXT
    width = HEADS * HEAD_DIM
    row_index = jnp.arange(devices, dtype=jnp.int32)[:, None] * jnp.ones((1, TOK_DEV), jnp.int32)
    inverse = jnp.zeros((devices, TOK_DEV), jnp.int32).at[row_index, plan].set(jnp.ones((devices, 1), jnp.int32) * jnp.arange(TOK_DEV, dtype=jnp.int32)[None, :])

    def to_home(stored):
        arrived = stored.reshape(devices, devices, share, width).transpose(1, 0, 2, 3).reshape(devices, TOK_DEV, width)
        placed = jnp.take_along_axis(arrived, inverse[:, :, None], axis=1)
        return placed.reshape(TOKENS // SPAN, SPAN, HEADS, HEAD_DIM)
    queries = to_home(q_store)
    keys_home = to_home(k_store)
    values_home = to_home(v_store)
    docs = doc_ids.reshape(TOKENS // SPAN, SPAN)
    causal = jnp.arange(SPAN)[:, None] >= jnp.arange(SPAN)[None, :]

    def advance(carry, block):
        query_block, key_block, value_block, doc_block = block
        qf = query_block.astype(jnp.float32)
        kf = key_block.astype(jnp.float32)
        vf = value_block.astype(jnp.float32)
        scores = jnp.einsum('thd,shd->hts', qf, kf)
        allowed = jnp.logical_and(causal, doc_block[:, None] == doc_block[None, :])
        weights = jnp.where(allowed[None], scores, jnp.zeros_like(scores)).astype(jnp.bfloat16)
        weights = lax.optimization_barrier(weights).astype(jnp.float32)
        inner = jnp.einsum('hts,she->the', weights, vf)
        carry_state, carry_doc = carry
        rounded = lax.optimization_barrier(carry_state.astype(jnp.bfloat16)).astype(jnp.float32)
        match = (doc_block == carry_doc[0]).astype(jnp.float32)
        carried = jnp.einsum('thd,hde->the', qf, rounded) * match[:, None, None]
        tail = (doc_block == doc_block[-1]).astype(jnp.float32)
        block_state = jnp.einsum('shd,she->hde', kf * tail[:, None, None], vf)
        updated = merge_states(carry, (block_state, doc_block[-1:]))
        return (updated, inner + carried)
    start = (jnp.zeros((HEADS, HEAD_DIM, HEAD_DIM), jnp.float32), jnp.full((1,), -1, jnp.int32))
    final, mixed = lax.scan(advance, start, (queries, keys_home, values_home, docs))
    scale = lax.rsqrt(lax.optimization_barrier(jnp.mean(mixed * mixed, axis=-1, keepdims=True)) + 1e-06)
    normed = (mixed * scale * gain.reshape(HEADS, HEAD_DIM)).astype(jnp.bfloat16)
    normed = normed.reshape(devices, TOK_DEV, width)
    leaving = jnp.take_along_axis(normed, plan[:, :, None], axis=1)
    return leaving.reshape(devices, devices, share, width).transpose(1, 0, 2, 3).reshape(TOKENS, width)
```

```python
import functools

import jax
import jax.numpy as jnp
from jax import lax
from jax.experimental import pallas as pl
from jax.experimental.pallas import tpu as pltpu
from jax.sharding import PartitionSpec as P

HEAD_DIM = 128
SPAN = 128
TILE = 16
MESH = pl.DeviceIdType.MESH


def flip(me, mask, n):
    out, bit = 0, 1
    while bit < n:
        mine, other = (me // bit) % 2, (mask // bit) % 2
        out = out + bit * (mine + other - 2 * mine * other)
        bit *= 2
    return out


def heads_kernel(
    n, heads, q_ref, k_ref, v_ref, plan_ref, docs_ref, gain_ref, out_ref,
    got, leaving, info, mask, tail, match, keep, send_sem, got_sem, info_sem, out_sem,
):
    tokens = q_ref.shape[0]
    share = tokens // n
    blocks = TILE // share
    rows = n * TILE
    chunks = tokens // TILE
    me = lax.axis_index("context")
    f32, bf16 = jnp.float32, jnp.bfloat16

    barrier = pltpu.get_barrier_semaphore()

    @pl.loop(1, n)
    def _(step):
        pl.semaphore_signal(
            barrier, inc=1, device_id={"context": flip(me, step, n)}, device_id_type=MESH
        )

    plan = plan_ref[...]
    here = lax.broadcasted_iota(jnp.int32, (tokens, tokens), 0) == plan
    docs = jnp.dot(
        jnp.broadcast_to(docs_ref[...], (8, tokens)).astype(f32).astype(bf16),
        here.astype(f32).astype(bf16),
        preferred_element_type=f32,
    )
    line = lax.broadcasted_iota(jnp.int32, (8, tokens), 0)
    lines = jnp.where(line == 0, jnp.broadcast_to(plan, (8, tokens)).astype(f32), docs)
    turn = me % blocks
    row = lax.broadcasted_iota(jnp.int32, (tokens, rows), 1)
    arrived = lax.broadcasted_iota(jnp.int32, (tokens, rows), 0)
    mine = (row % TILE) // share == turn
    spread = jnp.logical_and(mine, (row // TILE) * share + row % share == arrived)
    spread_lines = jnp.dot(
        lines.astype(bf16), spread.astype(f32).astype(bf16), preferred_element_type=f32
    )
    base = jnp.where(
        jnp.logical_and(mine[:8], lax.broadcasted_iota(jnp.int32, (8, rows), 0) == 0),
        (turn * tokens).astype(f32),
        0.0,
    )
    info[me] = spread_lines + base

    pl.semaphore_wait(barrier, n - 1)

    @pl.loop(1, n)
    def _(step):
        to = flip(me, step, n)
        pltpu.make_async_remote_copy(
            src_ref=info.at[me], dst_ref=info.at[me],
            send_sem=info_sem.at[0], recv_sem=info_sem.at[1],
            device_id={"context": to}, device_id_type=MESH,
        ).start()

    def columns(device, g):
        return pl.ds(pl.multiple_of((device * heads + g) * HEAD_DIM, HEAD_DIM), HEAD_DIM)

    for g in range(heads):

        @pl.loop(1, n)
        def _(step, g=g):
            to = flip(me, (step * 7) % n, n)
            for a, ref in enumerate((q_ref, k_ref, v_ref)):
                pltpu.make_async_remote_copy(
                    src_ref=ref.at[:, columns(to, g)], dst_ref=got.at[g, a, me],
                    send_sem=send_sem.at[g], recv_sem=got_sem.at[g],
                    device_id={"context": to}, device_id_type=MESH,
                ).start()

        for a, ref in enumerate((q_ref, k_ref, v_ref)):
            pltpu.make_async_copy(
                ref.at[:, columns(me, g)], got.at[g, a, me], got_sem.at[g]
            ).start()

    def wait_for(ref, sem):
        pltpu.make_async_copy(ref, ref, sem).wait()

    wait_for(info.at[pl.ds(0, n - 1)], info_sem.at[1])
    last = jnp.full((1, 1), -1.0, f32)
    for c in range(chunks):
        lines = info[c * blocks]
        for b in range(1, blocks):
            lines = lines + info[c * blocks + b]
        upright = lines.T
        at_row, doc_row = lines[0:1], lines[1:2]
        at_col, doc_col = upright[:, 0:1], upright[:, 1:2]
        allowed = jnp.logical_and(at_row <= at_col, doc_row == doc_col)
        mask[c] = jnp.where(allowed, 1.0, 0.0).astype(bf16)
        doc_wide = jnp.broadcast_to(doc_col, (rows, HEAD_DIM))
        match[c] = jnp.where(doc_wide == last, 1.0, 0.0).astype(bf16)
        latest = jnp.max(doc_row, axis=1, keepdims=True)
        tail[c] = jnp.where(doc_wide == latest, 1.0, 0.0).astype(bf16)
        keep[c] = jnp.broadcast_to(jnp.where(last == latest, 1.0, 0.0), (8, HEAD_DIM))
        last = latest

    for g in range(heads):
        wait_for(got.at[g], got_sem.at[g])
        gain = gain_ref[pl.ds(me * heads + g, 1), :]
        state = jnp.zeros((HEAD_DIM, HEAD_DIM), f32)
        for c in range(chunks):
            part = pl.ds(c * TILE, TILE)
            q = got[g, 0, :, part, :].reshape(rows, HEAD_DIM)
            k = got[g, 1, :, part, :].reshape(rows, HEAD_DIM)
            v = got[g, 2, :, part, :].reshape(rows, HEAD_DIM)
            scores = lax.dot_general(q, k, (((1,), (1,)), ((), ())), preferred_element_type=f32)
            weights = scores.astype(bf16) * mask[c]
            mixed = jnp.dot(weights, v, preferred_element_type=f32)
            if c:
                mixed = mixed + jnp.dot(
                    q * match[c], state.astype(bf16), preferred_element_type=f32
                )
            if c < chunks - 1:
                state = state * keep[c, 0:1] + lax.dot_general(
                    k * tail[c], v, (((0,), (0,)), ((), ())), preferred_element_type=f32
                )
            scale = lax.rsqrt(jnp.mean(mixed * mixed, axis=-1, keepdims=True) + 1e-06)
            leaving[g, :, part, :] = (
                (mixed * scale * gain).astype(bf16).reshape(n, TILE, HEAD_DIM)
            )

        @pl.loop(1, n)
        def _(step, g=g):
            to = flip(me, (step * 7) % n, n)
            pltpu.make_async_remote_copy(
                src_ref=leaving.at[g, to], dst_ref=out_ref.at[:, columns(me, g)],
                send_sem=send_sem.at[heads + g], recv_sem=out_sem.at[g],
                device_id={"context": to}, device_id_type=MESH,
            ).start()

        pltpu.make_async_copy(
            leaving.at[g, me], out_ref.at[:, columns(me, g)], out_sem.at[g]
        ).start()

    wait_for(info.at[pl.ds(0, n - 1)], info_sem.at[0])
    for g in range(heads):
        wait_for(got.at[g, :, pl.ds(0, n - 1)], send_sem.at[g])
        wait_for(leaving.at[g, pl.ds(0, n - 1)], send_sem.at[heads + g])
        wait_for(leaving.at[g], out_sem.at[g])


def by_heads(n, q_store, k_store, v_store, plan, doc_ids, gain):
    tokens, width = q_store.shape
    heads = width // HEAD_DIM // n
    rows, chunks = n * TILE, tokens // TILE
    bf16, f32 = jnp.bfloat16, jnp.float32
    return pl.pallas_call(
        functools.partial(heads_kernel, n, heads),
        out_shape=jax.ShapeDtypeStruct((tokens, width), bf16),
        in_specs=[pl.BlockSpec(memory_space=pltpu.VMEM)] * 6,
        out_specs=pl.BlockSpec(memory_space=pltpu.VMEM),
        scratch_shapes=[
            pltpu.VMEM((heads, 3, n, tokens, HEAD_DIM), bf16),
            pltpu.VMEM((heads, n, tokens, HEAD_DIM), bf16),
            pltpu.VMEM((n, 8, rows), f32),
            pltpu.VMEM((chunks, rows, rows), bf16),
            pltpu.VMEM((chunks, rows, HEAD_DIM), bf16),
            pltpu.VMEM((chunks, rows, HEAD_DIM), bf16),
            pltpu.VMEM((chunks, 8, HEAD_DIM), f32),
            pltpu.SemaphoreType.DMA((2 * heads,)),
            pltpu.SemaphoreType.DMA((heads,)),
            pltpu.SemaphoreType.DMA((2,)),
            pltpu.SemaphoreType.DMA((heads,)),
        ],
        compiler_params=pltpu.CompilerParams(
            collective_id=0, has_side_effects=True, vmem_limit_bytes=40 * 1024 * 1024
        ),
        cost_estimate=pl.CostEstimate(
            flops=2 * heads * n * tokens * HEAD_DIM * (2 * rows + 2 * HEAD_DIM),
            bytes_accessed=8 * tokens * width,
            transcendentals=heads * n * tokens,
        ),
    )(
        q_store, k_store, v_store, plan.reshape(1, tokens), doc_ids.reshape(1, tokens),
        gain.reshape(width // HEAD_DIM, HEAD_DIM),
    )


def entering(part, axis, combine, identity):
    place = lax.axis_index(axis)
    gathered = jax.tree.map(lambda a: lax.all_gather(a, axis), part)
    state = jax.tree.map(lambda a, e: jnp.zeros_like(a) + jnp.asarray(e, a.dtype), part, identity)

    def one(lap, state):
        return combine(
            state, jax.tree.map(lambda a: lax.dynamic_index_in_dim(a, lap, 0, False), gathered)
        )

    return lax.fori_loop(0, place, one, state)


def merge_states(earlier, later):
    early_state, early_doc = earlier
    late_state, late_doc = later
    keep_early = jnp.logical_or(early_doc == late_doc, late_doc < 0)
    merged = late_state + jnp.where(
        keep_early[:, None, None], early_state, jnp.zeros_like(early_state)
    )
    return (merged, jnp.where(late_doc < 0, early_doc, late_doc))


def by_positions(q_store, k_store, v_store, plan, doc_ids, gain):
    token_count = q_store.shape[0]
    head_count = q_store.shape[1] // HEAD_DIM
    span_count = token_count // SPAN
    placed = plan.reshape(-1)
    inverse = (
        jnp.zeros((token_count,), jnp.int32)
        .at[placed]
        .set(jnp.arange(token_count, dtype=jnp.int32))
    )

    def settle(arrived):
        return jnp.take(arrived, inverse, axis=0).reshape(span_count, SPAN, head_count, HEAD_DIM)

    docs = doc_ids.reshape(span_count, SPAN)
    last_doc = docs[:, -1]
    query_rows, key_rows, value_rows = (
        lax.all_to_all(q_store, "context", split_axis=0, concat_axis=0, tiled=True),
        lax.all_to_all(k_store, "context", split_axis=0, concat_axis=0, tiled=True),
        lax.all_to_all(v_store, "context", split_axis=0, concat_axis=0, tiled=True),
    )
    keys_home = settle(key_rows)
    values_home = settle(value_rows)
    tail_mask = (docs == last_doc[:, None]).astype(jnp.bfloat16)
    span_states = jnp.einsum(
        "cshd,cshe->chde",
        keys_home * tail_mask[:, :, None, None],
        values_home,
        preferred_element_type=jnp.float32,
    )
    device_part = (span_states[0], last_doc)
    identity = (jnp.zeros_like(span_states[0]), jnp.full((1,), -1, jnp.int32))
    running = entering(device_part, "context", merge_states, identity)
    carry_list = [running[0].astype(jnp.bfloat16)]
    doc_list = running[1]
    carry_states = jnp.stack(carry_list)
    queries = settle(query_rows)
    causal = jnp.arange(SPAN)[:, None] >= jnp.arange(SPAN)[None, :]
    allowed = jnp.logical_and(causal[None], docs[:, :, None] == docs[:, None, :])
    scores = jnp.einsum("cthd,cshd->chts", queries, keys_home, preferred_element_type=jnp.float32)
    weights = jnp.where(allowed[:, None], scores, 0.0).astype(jnp.bfloat16)
    inner = jnp.einsum("chts,cshe->cthe", weights, values_home, preferred_element_type=jnp.float32)
    match = (docs == doc_list[:, None]).astype(jnp.bfloat16)
    matched = queries * match[:, :, None, None]
    carried = jnp.einsum(
        "cthd,chde->cthe", matched, carry_states, preferred_element_type=jnp.float32
    )
    mixed = inner + carried
    scale = lax.rsqrt(jnp.mean(mixed * mixed, axis=-1, keepdims=True) + 1e-06)
    normed = (mixed * scale * gain.reshape(head_count, HEAD_DIM)).astype(jnp.bfloat16)
    normed = normed.reshape(token_count, head_count * HEAD_DIM)
    leaving = jnp.take(normed, placed, axis=0)
    return lax.all_to_all(leaving, "context", split_axis=0, concat_axis=0, tiled=True)


def solution(mesh):
    n = mesh.shape["context"]

    def on_device(q_store, k_store, v_store, plan, doc_ids, gain):
        tokens, width = q_store.shape
        head_count = width // HEAD_DIM
        share = tokens // n
        whole = head_count % n == 0 and n & (n - 1) == 0 and n > 1
        if whole and tokens % TILE == 0 and 0 < share <= TILE and TILE % share == 0:
            return by_heads(n, q_store, k_store, v_store, plan, doc_ids, gain)
        return by_positions(q_store, k_store, v_store, plan, doc_ids, gain)

    rows = P(("groups", "context"), None)
    return jax.shard_map(
        on_device,
        mesh=mesh,
        in_specs=(rows, rows, rows, rows, P(("groups", "context")), P()),
        out_specs=rows,
        check_vma=False,
    )
```

```python
import functools

import jax
import jax.numpy as jnp
from jax import lax
from jax.experimental import pallas as pl
from jax.experimental.pallas import tpu as pltpu
from jax.sharding import PartitionSpec as P

HEAD_DIM = 128
SPAN = 128
TILE = 16
MESH = pl.DeviceIdType.MESH


def flip(me, mask, n):
    out, bit = 0, 1
    while bit < n:
        mine, other = (me // bit) % 2, (mask // bit) % 2
        out = out + bit * (mine + other - 2 * mine * other)
        bit *= 2
    return out


def heads_kernel(
    n, heads, q_hbm, k_hbm, v_hbm, plan_hbm, docs_hbm, gain_hbm, out_ref,
    plan_ref, docs_ref, gain_ref, packed, got, leaving, info, mask, tail, match, keep,
    load_sem, small_sem, send_sem, got_sem, info_sem, out_sem,
):
    tokens = q_hbm.shape[0]
    share = tokens // n
    blocks = TILE // share
    rows = n * TILE
    chunks = tokens // TILE
    me = lax.axis_index("context")
    f32, bf16 = jnp.float32, jnp.bfloat16
    stride = n // 2 + 1 if n > 2 else 1

    def partner(step):
        return flip(me, (step * stride) % n, n)

    def columns(device, g):
        return pl.ds(pl.multiple_of((device * heads + g) * HEAD_DIM, HEAD_DIM), HEAD_DIM)

    def load(g):
        @pl.loop(1, n)
        def _(step):
            to = partner(step)
            for a, ref in enumerate((q_hbm, k_hbm, v_hbm)):
                pltpu.make_async_copy(
                    ref.at[:, columns(to, g)], packed.at[g, to, a], load_sem.at[g, to]
                ).start()

    def send(g):
        @pl.loop(1, n)
        def _(step):
            to = partner(step)
            pltpu.make_async_copy(packed.at[g, to], packed.at[g, to], load_sem.at[g, to]).wait()
            pltpu.make_async_remote_copy(
                src_ref=packed.at[g, to], dst_ref=got.at[g, me],
                send_sem=send_sem.at[g], recv_sem=got_sem.at[g],
                device_id={"context": to}, device_id_type=MESH,
            ).start()

    def own(g):
        for a, ref in enumerate((q_hbm, k_hbm, v_hbm)):
            pltpu.make_async_copy(
                ref.at[:, columns(me, g)], got.at[g, me, a], got_sem.at[g]
            ).start()

    barrier = pltpu.get_barrier_semaphore()

    @pl.loop(1, n)
    def _(step):
        pl.semaphore_signal(
            barrier, inc=1, device_id={"context": partner(step)}, device_id_type=MESH
        )

    load(0)
    small = [
        pltpu.make_async_copy(source, target, small_sem.at[i])
        for i, (source, target) in enumerate(
            ((plan_hbm, plan_ref), (docs_hbm, docs_ref), (gain_hbm, gain_ref))
        )
    ]
    for copy in small:
        copy.start()

    pl.semaphore_wait(barrier, n - 1)
    send(0)
    for g in range(1, heads):
        load(g)
    for g in range(heads):
        own(g)
    for copy in small:
        copy.wait()

    plan = plan_ref[...]
    here = lax.broadcasted_iota(jnp.int32, (tokens, tokens), 0) == plan
    docs = jnp.dot(
        jnp.broadcast_to(docs_ref[...], (8, tokens)).astype(f32).astype(bf16),
        here.astype(f32).astype(bf16),
        preferred_element_type=f32,
    )
    line = lax.broadcasted_iota(jnp.int32, (8, tokens), 0)
    lines = jnp.where(line == 0, jnp.broadcast_to(plan, (8, tokens)).astype(f32), docs)
    turn = me % blocks
    row = lax.broadcasted_iota(jnp.int32, (tokens, rows), 1)
    arrived = lax.broadcasted_iota(jnp.int32, (tokens, rows), 0)
    mine = (row % TILE) // share == turn
    spread = jnp.logical_and(mine, (row // TILE) * share + row % share == arrived)
    spread_lines = jnp.dot(
        lines.astype(bf16), spread.astype(f32).astype(bf16), preferred_element_type=f32
    )
    base = jnp.where(
        jnp.logical_and(mine[:8], lax.broadcasted_iota(jnp.int32, (8, rows), 0) == 0),
        (turn * tokens).astype(f32),
        0.0,
    )
    info[me] = spread_lines + base

    @pl.loop(1, n)
    def _(step):
        pltpu.make_async_remote_copy(
            src_ref=info.at[me], dst_ref=info.at[me],
            send_sem=info_sem.at[0], recv_sem=info_sem.at[1],
            device_id={"context": partner(step)}, device_id_type=MESH,
        ).start()

    for g in range(1, heads):
        send(g)

    def wait_for(ref, sem):
        pltpu.make_async_copy(ref, ref, sem).wait()

    wait_for(info.at[pl.ds(0, n - 1)], info_sem.at[1])
    last = jnp.full((1, 1), -1.0, f32)
    for c in range(chunks):
        lines = info[c * blocks]
        for b in range(1, blocks):
            lines = lines + info[c * blocks + b]
        upright = lines.T
        at_row, doc_row = lines[0:1], lines[1:2]
        at_col, doc_col = upright[:, 0:1], upright[:, 1:2]
        allowed = jnp.logical_and(at_row <= at_col, doc_row == doc_col)
        mask[c] = jnp.where(allowed, 1.0, 0.0).astype(bf16)
        doc_wide = jnp.broadcast_to(doc_col, (rows, HEAD_DIM))
        match[c] = jnp.where(doc_wide == last, 1.0, 0.0).astype(bf16)
        latest = jnp.max(doc_row, axis=1, keepdims=True)
        tail[c] = jnp.where(doc_wide == latest, 1.0, 0.0).astype(bf16)
        keep[c] = jnp.broadcast_to(jnp.where(last == latest, 1.0, 0.0), (8, HEAD_DIM))
        last = latest

    for g in range(heads):
        wait_for(got.at[g], got_sem.at[g])
        gain = gain_ref[pl.ds(me * heads + g, 1), :]
        state = jnp.zeros((HEAD_DIM, HEAD_DIM), f32)
        for c in range(chunks):
            part = pl.ds(c * TILE, TILE)
            q = got[g, :, 0, part, :].reshape(rows, HEAD_DIM)
            k = got[g, :, 1, part, :].reshape(rows, HEAD_DIM)
            v = got[g, :, 2, part, :].reshape(rows, HEAD_DIM)
            scores = lax.dot_general(q, k, (((1,), (1,)), ((), ())), preferred_element_type=f32)
            weights = scores.astype(bf16) * mask[c]
            mixed = jnp.dot(weights, v, preferred_element_type=f32)
            if c:
                mixed = mixed + jnp.dot(
                    q * match[c], state.astype(bf16), preferred_element_type=f32
                )
            if c < chunks - 1:
                state = state * keep[c, 0:1] + lax.dot_general(
                    k * tail[c], v, (((0,), (0,)), ((), ())), preferred_element_type=f32
                )
            scale = lax.rsqrt(jnp.mean(mixed * mixed, axis=-1, keepdims=True) + 1e-06)
            leaving[g, :, part, :] = (
                (mixed * scale * gain).astype(bf16).reshape(n, TILE, HEAD_DIM)
            )

        @pl.loop(1, n)
        def _(step, g=g):
            to = partner(step)
            pltpu.make_async_remote_copy(
                src_ref=leaving.at[g, to], dst_ref=out_ref.at[:, columns(me, g)],
                send_sem=send_sem.at[heads + g], recv_sem=out_sem.at[g],
                device_id={"context": to}, device_id_type=MESH,
            ).start()

        pltpu.make_async_copy(
            leaving.at[g, me], out_ref.at[:, columns(me, g)], out_sem.at[g]
        ).start()

    wait_for(info.at[pl.ds(0, n - 1)], info_sem.at[0])
    for g in range(heads):
        wait_for(got.at[g, pl.ds(0, n - 1)], send_sem.at[g])
        wait_for(leaving.at[g, pl.ds(0, n - 1)], send_sem.at[heads + g])
        wait_for(leaving.at[g], out_sem.at[g])


def by_heads(n, q_store, k_store, v_store, plan, doc_ids, gain):
    tokens, width = q_store.shape
    heads = width // HEAD_DIM // n
    rows, chunks = n * TILE, tokens // TILE
    bf16, f32 = jnp.bfloat16, jnp.float32
    return pl.pallas_call(
        functools.partial(heads_kernel, n, heads),
        out_shape=jax.ShapeDtypeStruct((tokens, width), bf16),
        in_specs=[pl.BlockSpec(memory_space=pltpu.HBM)] * 6,
        out_specs=pl.BlockSpec(memory_space=pltpu.HBM),
        scratch_shapes=[
            pltpu.VMEM((1, tokens), jnp.int32),
            pltpu.VMEM((1, tokens), jnp.int32),
            pltpu.VMEM((width // HEAD_DIM, HEAD_DIM), f32),
            pltpu.VMEM((heads, n, 3, tokens, HEAD_DIM), bf16),
            pltpu.VMEM((heads, n, 3, tokens, HEAD_DIM), bf16),
            pltpu.VMEM((heads, n, tokens, HEAD_DIM), bf16),
            pltpu.VMEM((n, 8, rows), f32),
            pltpu.VMEM((chunks, rows, rows), bf16),
            pltpu.VMEM((chunks, rows, HEAD_DIM), bf16),
            pltpu.VMEM((chunks, rows, HEAD_DIM), bf16),
            pltpu.VMEM((chunks, 8, HEAD_DIM), f32),
            pltpu.SemaphoreType.DMA((heads, n)),
            pltpu.SemaphoreType.DMA((3,)),
            pltpu.SemaphoreType.DMA((2 * heads,)),
            pltpu.SemaphoreType.DMA((heads,)),
            pltpu.SemaphoreType.DMA((2,)),
            pltpu.SemaphoreType.DMA((heads,)),
        ],
        compiler_params=pltpu.CompilerParams(
            collective_id=0, has_side_effects=True, vmem_limit_bytes=63 * 1024 * 1024
        ),
        cost_estimate=pl.CostEstimate(
            flops=2 * heads * n * tokens * HEAD_DIM * (2 * rows + 2 * HEAD_DIM),
            bytes_accessed=8 * tokens * width,
            transcendentals=heads * n * tokens,
        ),
    )(
        q_store, k_store, v_store, plan.reshape(1, tokens), doc_ids.reshape(1, tokens),
        gain.reshape(width // HEAD_DIM, HEAD_DIM),
    )


def entering(part, axis, combine, identity):
    place = lax.axis_index(axis)
    gathered = jax.tree.map(lambda a: lax.all_gather(a, axis), part)
    state = jax.tree.map(lambda a, e: jnp.zeros_like(a) + jnp.asarray(e, a.dtype), part, identity)

    def one(lap, state):
        return combine(
            state, jax.tree.map(lambda a: lax.dynamic_index_in_dim(a, lap, 0, False), gathered)
        )

    return lax.fori_loop(0, place, one, state)


def merge_states(earlier, later):
    early_state, early_doc = earlier
    late_state, late_doc = later
    keep_early = jnp.logical_or(early_doc == late_doc, late_doc < 0)
    merged = late_state + jnp.where(
        keep_early[:, None, None], early_state, jnp.zeros_like(early_state)
    )
    return (merged, jnp.where(late_doc < 0, early_doc, late_doc))


def by_positions(q_store, k_store, v_store, plan, doc_ids, gain):
    token_count = q_store.shape[0]
    head_count = q_store.shape[1] // HEAD_DIM
    span_count = token_count // SPAN
    placed = plan.reshape(-1)
    inverse = (
        jnp.zeros((token_count,), jnp.int32)
        .at[placed]
        .set(jnp.arange(token_count, dtype=jnp.int32))
    )

    def settle(arrived):
        return jnp.take(arrived, inverse, axis=0).reshape(span_count, SPAN, head_count, HEAD_DIM)

    docs = doc_ids.reshape(span_count, SPAN)
    last_doc = docs[:, -1]
    query_rows, key_rows, value_rows = (
        lax.all_to_all(q_store, "context", split_axis=0, concat_axis=0, tiled=True),
        lax.all_to_all(k_store, "context", split_axis=0, concat_axis=0, tiled=True),
        lax.all_to_all(v_store, "context", split_axis=0, concat_axis=0, tiled=True),
    )
    keys_home = settle(key_rows)
    values_home = settle(value_rows)
    tail_mask = (docs == last_doc[:, None]).astype(jnp.bfloat16)
    span_states = jnp.einsum(
        "cshd,cshe->chde",
        keys_home * tail_mask[:, :, None, None],
        values_home,
        preferred_element_type=jnp.float32,
    )
    device_part = (span_states[0], last_doc)
    identity = (jnp.zeros_like(span_states[0]), jnp.full((1,), -1, jnp.int32))
    running = entering(device_part, "context", merge_states, identity)
    carry_list = [running[0].astype(jnp.bfloat16)]
    doc_list = running[1]
    carry_states = jnp.stack(carry_list)
    queries = settle(query_rows)
    causal = jnp.arange(SPAN)[:, None] >= jnp.arange(SPAN)[None, :]
    allowed = jnp.logical_and(causal[None], docs[:, :, None] == docs[:, None, :])
    scores = jnp.einsum("cthd,cshd->chts", queries, keys_home, preferred_element_type=jnp.float32)
    weights = jnp.where(allowed[:, None], scores, 0.0).astype(jnp.bfloat16)
    inner = jnp.einsum("chts,cshe->cthe", weights, values_home, preferred_element_type=jnp.float32)
    match = (docs == doc_list[:, None]).astype(jnp.bfloat16)
    matched = queries * match[:, :, None, None]
    carried = jnp.einsum(
        "cthd,chde->cthe", matched, carry_states, preferred_element_type=jnp.float32
    )
    mixed = inner + carried
    scale = lax.rsqrt(jnp.mean(mixed * mixed, axis=-1, keepdims=True) + 1e-06)
    normed = (mixed * scale * gain.reshape(head_count, HEAD_DIM)).astype(jnp.bfloat16)
    normed = normed.reshape(token_count, head_count * HEAD_DIM)
    leaving = jnp.take(normed, placed, axis=0)
    return lax.all_to_all(leaving, "context", split_axis=0, concat_axis=0, tiled=True)


def solution(mesh):
    n = mesh.shape["context"]

    def on_device(q_store, k_store, v_store, plan, doc_ids, gain):
        tokens, width = q_store.shape
        head_count = width // HEAD_DIM
        share = tokens // n
        whole = head_count % n == 0 and n & (n - 1) == 0 and n > 1
        if whole and tokens % TILE == 0 and 0 < share <= TILE and TILE % share == 0:
            return by_heads(n, q_store, k_store, v_store, plan, doc_ids, gain)
        return by_positions(q_store, k_store, v_store, plan, doc_ids, gain)

    rows = P(("groups", "context"), None)
    return jax.shard_map(
        on_device,
        mesh=mesh,
        in_specs=(rows, rows, rows, rows, P(("groups", "context")), P()),
        out_specs=rows,
        check_vma=False,
    )
```

```python
import functools

import jax
import jax.numpy as jnp
from jax import lax
from jax.experimental import pallas as pl
from jax.experimental.pallas import tpu as pltpu
from jax.sharding import PartitionSpec as P

HEAD_DIM = 128
SPAN = 128
TILE = 16
MESH = pl.DeviceIdType.MESH


def flip(me, mask, n):
    out, bit = 0, 1
    while bit < n:
        mine, other = (me // bit) % 2, (mask // bit) % 2
        out = out + bit * (mine + other - 2 * mine * other)
        bit *= 2
    return out


def heads_kernel(
    n, heads, q_hbm, k_hbm, v_hbm, plan_hbm, docs_hbm, gain_hbm, out_ref,
    plan_ref, docs_ref, gain_ref, packed, got, leaving, info, mask, tail, match, keep,
    load_sem, small_sem, send_sem, got_sem, info_sem, out_sem,
):
    tokens = q_hbm.shape[0]
    share = tokens // n
    blocks = TILE // share
    rows = n * TILE
    chunks = tokens // TILE
    me = lax.axis_index("context")
    f32, bf16 = jnp.float32, jnp.bfloat16
    stride = n // 2 + 1 if n > 2 else 1

    def partner(step):
        return flip(me, (step * stride) % n, n)

    def columns(device, g):
        return pl.ds(pl.multiple_of((device * heads + g) * HEAD_DIM, HEAD_DIM), HEAD_DIM)

    def load(g):
        @pl.loop(1, n)
        def _(step):
            to = partner(step)
            for a, ref in enumerate((q_hbm, k_hbm, v_hbm)):
                pltpu.make_async_copy(
                    ref.at[:, columns(to, g)], packed.at[g, to, a], load_sem.at[g, to]
                ).start()

    def send(g):
        @pl.loop(1, n)
        def _(step):
            to = partner(step)
            pltpu.make_async_copy(packed.at[g, to], packed.at[g, to], load_sem.at[g, to]).wait()
            pltpu.make_async_remote_copy(
                src_ref=packed.at[g, to], dst_ref=got.at[g, me],
                send_sem=send_sem.at[g], recv_sem=got_sem.at[g],
                device_id={"context": to}, device_id_type=MESH,
            ).start()

    def own(g):
        for a, ref in enumerate((q_hbm, k_hbm, v_hbm)):
            pltpu.make_async_copy(
                ref.at[:, columns(me, g)], got.at[g, me, a], got_sem.at[g]
            ).start()

    barrier = pltpu.get_barrier_semaphore()

    @pl.loop(1, n)
    def _(step):
        pl.semaphore_signal(
            barrier, inc=1, device_id={"context": partner(step)}, device_id_type=MESH
        )

    load(0)
    small = [
        pltpu.make_async_copy(source, target, small_sem.at[i])
        for i, (source, target) in enumerate(
            ((plan_hbm, plan_ref), (docs_hbm, docs_ref), (gain_hbm, gain_ref))
        )
    ]
    for copy in small:
        copy.start()

    pl.semaphore_wait(barrier, n - 1)
    send(0)
    for g in range(1, heads):
        load(g)
    for g in range(heads):
        own(g)
    for copy in small:
        copy.wait()

    plan = plan_ref[...]
    here = lax.broadcasted_iota(jnp.int32, (tokens, tokens), 0) == plan
    docs = jnp.dot(
        jnp.broadcast_to(docs_ref[...], (8, tokens)).astype(f32).astype(bf16),
        here.astype(f32).astype(bf16),
        preferred_element_type=f32,
    )
    line = lax.broadcasted_iota(jnp.int32, (8, tokens), 0)
    lines = jnp.where(line == 0, jnp.broadcast_to(plan, (8, tokens)).astype(f32), docs)
    turn = me % blocks
    row = lax.broadcasted_iota(jnp.int32, (tokens, rows), 1)
    arrived = lax.broadcasted_iota(jnp.int32, (tokens, rows), 0)
    mine = (row % TILE) // share == turn
    spread = jnp.logical_and(mine, (row // TILE) * share + row % share == arrived)
    spread_lines = jnp.dot(
        lines.astype(bf16), spread.astype(f32).astype(bf16), preferred_element_type=f32
    )
    base = jnp.where(
        jnp.logical_and(mine[:8], lax.broadcasted_iota(jnp.int32, (8, rows), 0) == 0),
        (turn * tokens).astype(f32),
        0.0,
    )
    info[me] = spread_lines + base

    @pl.loop(1, n)
    def _(step):
        pltpu.make_async_remote_copy(
            src_ref=info.at[me], dst_ref=info.at[me],
            send_sem=info_sem.at[0], recv_sem=info_sem.at[1],
            device_id={"context": partner(step)}, device_id_type=MESH,
        ).start()

    for g in range(1, heads):
        send(g)

    def wait_for(ref, sem):
        pltpu.make_async_copy(ref, ref, sem).wait()

    wait_for(info.at[pl.ds(0, n - 1)], info_sem.at[1])
    last = jnp.full((1, 1), -1.0, f32)
    for c in range(chunks):
        lines = info[c * blocks]
        for b in range(1, blocks):
            lines = lines + info[c * blocks + b]
        upright = lines.T
        at_row, doc_row = lines[0:1], lines[1:2]
        at_col, doc_col = upright[:, 0:1], upright[:, 1:2]
        allowed = jnp.logical_and(at_row <= at_col, doc_row == doc_col)
        mask[c] = jnp.where(allowed, 1.0, 0.0).astype(bf16)
        doc_wide = jnp.broadcast_to(doc_col, (rows, HEAD_DIM))
        match[c] = jnp.where(doc_wide == last, 1.0, 0.0).astype(bf16)
        latest = jnp.max(doc_row, axis=1, keepdims=True)
        tail[c] = jnp.where(doc_wide == latest, 1.0, 0.0).astype(bf16)
        keep[c] = jnp.broadcast_to(jnp.where(last == latest, 1.0, 0.0), (8, HEAD_DIM))
        last = latest

    for g in range(heads):
        wait_for(got.at[g], got_sem.at[g])
        gain = gain_ref[pl.ds(me * heads + g, 1), :]
        state = jnp.zeros((HEAD_DIM, HEAD_DIM), f32)
        for c in range(chunks):
            part = pl.ds(c * TILE, TILE)
            q = got[g, :, 0, part, :].reshape(rows, HEAD_DIM)
            k = got[g, :, 1, part, :].reshape(rows, HEAD_DIM)
            v = got[g, :, 2, part, :].reshape(rows, HEAD_DIM)
            scores = lax.dot_general(q, k, (((1,), (1,)), ((), ())), preferred_element_type=f32)
            weights = scores.astype(bf16) * mask[c]
            mixed = jnp.dot(weights, v, preferred_element_type=f32)
            if c:
                mixed = mixed + jnp.dot(
                    q * match[c], state.astype(bf16), preferred_element_type=f32
                )
            if c < chunks - 1:
                state = state * keep[c, 0:1] + lax.dot_general(
                    k * tail[c], v, (((0,), (0,)), ((), ())), preferred_element_type=f32
                )
            scale = lax.rsqrt(jnp.mean(mixed * mixed, axis=-1, keepdims=True) + 1e-06)
            leaving[g, :, part, :] = (
                (mixed * scale * gain).astype(bf16).reshape(n, TILE, HEAD_DIM)
            )

        @pl.loop(1, n)
        def _(step, g=g):
            to = partner(step)
            pltpu.make_async_remote_copy(
                src_ref=leaving.at[g, to], dst_ref=out_ref.at[:, columns(me, g)],
                send_sem=send_sem.at[heads + g], recv_sem=out_sem.at[g],
                device_id={"context": to}, device_id_type=MESH,
            ).start()

        pltpu.make_async_copy(
            leaving.at[g, me], out_ref.at[:, columns(me, g)], out_sem.at[g]
        ).start()

    wait_for(info.at[pl.ds(0, n - 1)], info_sem.at[0])
    for g in range(heads):
        wait_for(got.at[g, pl.ds(0, n - 1)], send_sem.at[g])
        wait_for(leaving.at[g, pl.ds(0, n - 1)], send_sem.at[heads + g])
        wait_for(leaving.at[g], out_sem.at[g])


def by_heads(n, q_store, k_store, v_store, plan, doc_ids, gain):
    tokens, width = q_store.shape
    heads = width // HEAD_DIM // n
    rows, chunks = n * TILE, tokens // TILE
    bf16, f32 = jnp.bfloat16, jnp.float32
    return pl.pallas_call(
        functools.partial(heads_kernel, n, heads),
        out_shape=jax.ShapeDtypeStruct((tokens, width), bf16),
        in_specs=[pl.BlockSpec(memory_space=pltpu.HBM)] * 6,
        out_specs=pl.BlockSpec(memory_space=pltpu.VMEM),
        scratch_shapes=[
            pltpu.VMEM((1, tokens), jnp.int32),
            pltpu.VMEM((1, tokens), jnp.int32),
            pltpu.VMEM((width // HEAD_DIM, HEAD_DIM), f32),
            pltpu.VMEM((heads, n, 3, tokens, HEAD_DIM), bf16),
            pltpu.VMEM((heads, n, 3, tokens, HEAD_DIM), bf16),
            pltpu.VMEM((heads, n, tokens, HEAD_DIM), bf16),
            pltpu.VMEM((n, 8, rows), f32),
            pltpu.VMEM((chunks, rows, rows), bf16),
            pltpu.VMEM((chunks, rows, HEAD_DIM), bf16),
            pltpu.VMEM((chunks, rows, HEAD_DIM), bf16),
            pltpu.VMEM((chunks, 8, HEAD_DIM), f32),
            pltpu.SemaphoreType.DMA((heads, n)),
            pltpu.SemaphoreType.DMA((3,)),
            pltpu.SemaphoreType.DMA((2 * heads,)),
            pltpu.SemaphoreType.DMA((heads,)),
            pltpu.SemaphoreType.DMA((2,)),
            pltpu.SemaphoreType.DMA((heads,)),
        ],
        compiler_params=pltpu.CompilerParams(
            collective_id=0, has_side_effects=True, vmem_limit_bytes=52 * 1024 * 1024
        ),
        cost_estimate=pl.CostEstimate(
            flops=2 * heads * n * tokens * HEAD_DIM * (2 * rows + 2 * HEAD_DIM),
            bytes_accessed=8 * tokens * width,
            transcendentals=heads * n * tokens,
        ),
    )(
        q_store, k_store, v_store, plan.reshape(1, tokens), doc_ids.reshape(1, tokens),
        gain.reshape(width // HEAD_DIM, HEAD_DIM),
    )


def entering(part, axis, combine, identity):
    place = lax.axis_index(axis)
    gathered = jax.tree.map(lambda a: lax.all_gather(a, axis), part)
    state = jax.tree.map(lambda a, e: jnp.zeros_like(a) + jnp.asarray(e, a.dtype), part, identity)

    def one(lap, state):
        return combine(
            state, jax.tree.map(lambda a: lax.dynamic_index_in_dim(a, lap, 0, False), gathered)
        )

    return lax.fori_loop(0, place, one, state)


def merge_states(earlier, later):
    early_state, early_doc = earlier
    late_state, late_doc = later
    keep_early = jnp.logical_or(early_doc == late_doc, late_doc < 0)
    merged = late_state + jnp.where(
        keep_early[:, None, None], early_state, jnp.zeros_like(early_state)
    )
    return (merged, jnp.where(late_doc < 0, early_doc, late_doc))


def by_positions(q_store, k_store, v_store, plan, doc_ids, gain):
    token_count = q_store.shape[0]
    head_count = q_store.shape[1] // HEAD_DIM
    span_count = token_count // SPAN
    placed = plan.reshape(-1)
    inverse = (
        jnp.zeros((token_count,), jnp.int32)
        .at[placed]
        .set(jnp.arange(token_count, dtype=jnp.int32))
    )

    def settle(arrived):
        return jnp.take(arrived, inverse, axis=0).reshape(span_count, SPAN, head_count, HEAD_DIM)

    docs = doc_ids.reshape(span_count, SPAN)
    last_doc = docs[:, -1]
    query_rows, key_rows, value_rows = (
        lax.all_to_all(q_store, "context", split_axis=0, concat_axis=0, tiled=True),
        lax.all_to_all(k_store, "context", split_axis=0, concat_axis=0, tiled=True),
        lax.all_to_all(v_store, "context", split_axis=0, concat_axis=0, tiled=True),
    )
    keys_home = settle(key_rows)
    values_home = settle(value_rows)
    tail_mask = (docs == last_doc[:, None]).astype(jnp.bfloat16)
    span_states = jnp.einsum(
        "cshd,cshe->chde",
        keys_home * tail_mask[:, :, None, None],
        values_home,
        preferred_element_type=jnp.float32,
    )
    device_part = (span_states[0], last_doc)
    identity = (jnp.zeros_like(span_states[0]), jnp.full((1,), -1, jnp.int32))
    running = entering(device_part, "context", merge_states, identity)
    carry_list = [running[0].astype(jnp.bfloat16)]
    doc_list = running[1]
    carry_states = jnp.stack(carry_list)
    queries = settle(query_rows)
    causal = jnp.arange(SPAN)[:, None] >= jnp.arange(SPAN)[None, :]
    allowed = jnp.logical_and(causal[None], docs[:, :, None] == docs[:, None, :])
    scores = jnp.einsum("cthd,cshd->chts", queries, keys_home, preferred_element_type=jnp.float32)
    weights = jnp.where(allowed[:, None], scores, 0.0).astype(jnp.bfloat16)
    inner = jnp.einsum("chts,cshe->cthe", weights, values_home, preferred_element_type=jnp.float32)
    match = (docs == doc_list[:, None]).astype(jnp.bfloat16)
    matched = queries * match[:, :, None, None]
    carried = jnp.einsum(
        "cthd,chde->cthe", matched, carry_states, preferred_element_type=jnp.float32
    )
    mixed = inner + carried
    scale = lax.rsqrt(jnp.mean(mixed * mixed, axis=-1, keepdims=True) + 1e-06)
    normed = (mixed * scale * gain.reshape(head_count, HEAD_DIM)).astype(jnp.bfloat16)
    normed = normed.reshape(token_count, head_count * HEAD_DIM)
    leaving = jnp.take(normed, placed, axis=0)
    return lax.all_to_all(leaving, "context", split_axis=0, concat_axis=0, tiled=True)


def solution(mesh):
    n = mesh.shape["context"]

    def on_device(q_store, k_store, v_store, plan, doc_ids, gain):
        tokens, width = q_store.shape
        head_count = width // HEAD_DIM
        share = tokens // n
        whole = head_count % n == 0 and n & (n - 1) == 0 and n > 1
        if whole and tokens % TILE == 0 and 0 < share <= TILE and TILE % share == 0:
            return by_heads(n, q_store, k_store, v_store, plan, doc_ids, gain)
        return by_positions(q_store, k_store, v_store, plan, doc_ids, gain)

    rows = P(("groups", "context"), None)
    return jax.shard_map(
        on_device,
        mesh=mesh,
        in_specs=(rows, rows, rows, rows, P(("groups", "context")), P()),
        out_specs=rows,
        check_vma=False,
    )
```
